32 devices in a mesh: span: 4 (over z), space: 8 (over y, x, core).
Axes of the slice: x: 2, y: 2, z: 4, core: 2. Of those that a mesh axis runs over, the one named last changes fastest.
Arguments:
- frames: bfloat16 [12, 8, 32, 512], P('span', 'space')
- counts: int32 [4], replicated, may hold values from 1 to 3, as said below
- gain_one: float32 [512], replicated, may hold values from 0.5 to 1.5
- offset_one: float32 [512], replicated, may hold values from -3 to 3
- kernel_one: bfloat16 [3, 3, 3, 512, 512], P(None, None, None, 'space'), may hold values from -0.0546875 to 0.0546875
- bias_one: float32 [512], replicated, may hold values from -2 to 2
- gain_two: float32 [512], replicated, may hold values from 0.5 to 1.5
- offset_two: float32 [512], replicated, may hold values from -3 to 3
- kernel_two: bfloat16 [3, 3, 3, 512, 512], P(None, None, None, 'space'), may hold values from -0.0546875 to 0.0546875
- bias_two: float32 [512], replicated, may hold values from -2 to 2
Outputs:
- decoded: bfloat16 [12, 8, 32, 512], P('span', 'space')
The draws below stay inside these ranges and needn't reach their ends.
Inputs may be any that keep to these rules, and one draw needn't show every extreme that they name: `counts`: each group's live frames fill its first slots; some group is full and some group has one live frame.
All inputs are finite; a program needn't handle non-finite values.
Results may differ from the reference program's by a relative error of at most 0.003.
Values may be sent and summed in bfloat16 or wider, within the bound.
A program may use at most 64 MiB of HBM per device.

```python
import math
import jax
import jax.numpy as jnp
from jax import lax

C = 512
GROUPS = 32
F_DEV = 3
W = 32
H = 8
FRAMES = 12
N_SPAN = 4


def draw_frames(key, part):
    key = jax.random.fold_in(key, 1)
    key_noise, key_cols = jax.random.split(key, 2)
    row_pos = jnp.arange(H, dtype=jnp.float32) / max(H - 1, 1)
    noise_all = jax.random.normal(key_noise, (FRAMES, H, W, C), jnp.float32)
    row_scale = 3.0 ** row_pos
    col_scale = jnp.exp(jax.random.uniform(key_cols, (W,), jnp.float32, 0.0, math.log(2.0)))
    return (noise_all * row_scale[None, :, None, None] * col_scale[None, None, :, None]).astype(jnp.bfloat16)


def draw_counts(key, part):
    key = jax.random.fold_in(key, 2)
    key_values, key_full = jax.random.split(key)
    values = jax.random.randint(key_values, (N_SPAN,), 1, F_DEV + 1, dtype=jnp.int32)
    full_group = jax.random.randint(key_full, (), 0, N_SPAN, dtype=jnp.int32)
    single_group = (full_group + 1) % N_SPAN
    group_ids = jnp.arange(N_SPAN, dtype=jnp.int32)
    values = jnp.where(group_ids == single_group, 1, values)
    values = jnp.where(group_ids == full_group, F_DEV, values)
    return values.astype(jnp.int32)


def levels(own_key, dims, cuts, least, largest):
    loudness = 1.0
    for axis_at, blocks in cuts:
        draws = jax.random.uniform(jax.random.fold_in(jax.random.fold_in(own_key, 6), axis_at), (blocks,), jnp.float32, least / len(cuts), largest / len(cuts))
        loudness = loudness * jnp.repeat(jnp.exp(draws), dims[axis_at] // blocks).reshape((-1,) + (1,) * (len(dims) - 1 - axis_at))
    return loudness


def gaussian(stream_key, dims, width, bound, pieces=(), kind=jnp.bfloat16):
    array = width * jax.random.normal(stream_key, dims, jnp.float32)
    if pieces:
        array = array * levels(stream_key, dims, pieces, -0.22, 0.18)
    return jnp.clip(array, -bound, bound).astype(kind)


def setup_inputs(seed: int = 0) -> dict:
    key_of = jax.random.split(jax.random.key(seed), 11)
    return {
        "frames": draw_frames(jax.random.fold_in(key_of[10], 71), 0),
        "counts": draw_counts(jax.random.fold_in(key_of[10], 71), 0),
        "gain_one": jnp.clip(1.0 + 0.1 * jax.random.normal(key_of[2], (C,), jnp.float32), 0.5, 1.5),
        "offset_one": gaussian(key_of[3], (C,), 0.5, 3.0, (), jnp.float32),
        "kernel_one": gaussian(key_of[4], (3, 3, 3, C, C), (27 * C) ** -0.5, 0.0546875, ((3, 8),)),
        "bias_one": gaussian(key_of[5], (C,), 0.3, 2.0, (), jnp.float32),
        "gain_two": jnp.clip(1.0 + 0.1 * jax.random.normal(key_of[6], (C,), jnp.float32), 0.5, 1.5),
        "offset_two": gaussian(key_of[7], (C,), 0.5, 3.0, (), jnp.float32),
        "kernel_two": gaussian(key_of[8], (3, 3, 3, C, C), (27 * C) ** -0.5, 0.0546875, ((3, 8),)),
        "bias_two": gaussian(key_of[9], (C,), 0.3, 2.0, (), jnp.float32),
    }


EPS = 1e-05

def norm_silu(values, gain_vec, offset_vec):
    grouped = values.reshape(values.shape[0], values.shape[1], GROUPS, -1)
    members = grouped.shape[0] * grouped.shape[1] * grouped.shape[3]
    average = lax.optimization_barrier(jnp.sum(grouped, axis=(0, 1, 3))) / members
    second_moment = lax.optimization_barrier(jnp.sum(grouped * grouped, axis=(0, 1, 3))) / members
    scale_now = lax.rsqrt(second_moment - average * average + EPS)
    normed = ((grouped - average[None, None, :, None]) * scale_now[None, None, :, None]).reshape(values.shape)
    return jax.nn.silu(normed * gain_vec + offset_vec).astype(jnp.bfloat16)

def causal_conv(normed, kernel, bias_vec, prev_one, prev_two):
    extended = jnp.concatenate([normed, jnp.zeros((1,) + normed.shape[1:], jnp.bfloat16)], 0)
    kernel_wide = kernel.astype(jnp.float32)
    slot_ids = jnp.arange(FRAMES, dtype=jnp.int32)
    pick_two = jnp.where(prev_two < 0, FRAMES, prev_two).astype(jnp.int32)
    pick_one = jnp.where(prev_one < 0, FRAMES, prev_one).astype(jnp.int32)

    def one_slot(chosen):
        window = jnp.stack([extended[chosen[0]], extended[chosen[1]], extended[chosen[2]]], 0).astype(jnp.float32)
        window = jnp.pad(window, ((0, 0), (1, 1), (1, 1), (0, 0)))
        summed = jnp.zeros((H * W, C), jnp.float32) + bias_vec[None, :]
        for time_off in range(3):
            for row_off in range(3):
                for col_off in range(3):
                    piece = window[time_off, row_off:row_off + H, col_off:col_off + W].reshape(H * W, C)
                    summed = summed + jnp.dot(piece, kernel_wide[time_off, row_off, col_off].T, precision=lax.Precision.HIGHEST)
        return summed.reshape(H, W, C).astype(jnp.bfloat16)
    return lax.map(one_slot, (pick_two, pick_one, slot_ids))

def reference(frames, counts, gain_one, offset_one, kernel_one, bias_one, gain_two, offset_two, kernel_two, bias_two):
    slot_ids = jnp.arange(FRAMES, dtype=jnp.int32)
    live_mask = slot_ids % F_DEV < counts[slot_ids // F_DEV]
    marker = jnp.where(live_mask, slot_ids, -1).astype(jnp.int32)
    latest = lax.cummax(marker, axis=0)
    prev_one = jnp.concatenate([jnp.full((1,), -1, jnp.int32), latest[:-1]])
    prev_two = jnp.where(prev_one >= 0, prev_one[jnp.maximum(prev_one, 0)], -1).astype(jnp.int32)
    live_float = live_mask.astype(jnp.float32)[:, None, None, None]
    normed_one = lax.map(lambda single: norm_silu(single.astype(jnp.float32), gain_one, offset_one), frames)
    normed_one = (normed_one.astype(jnp.float32) * live_float).astype(jnp.bfloat16)
    conv_one = causal_conv(normed_one, kernel_one, bias_one, prev_one, prev_two)
    normed_two = lax.map(lambda single: norm_silu(single.astype(jnp.float32), gain_two, offset_two), conv_one)
    normed_two = (normed_two.astype(jnp.float32) * live_float).astype(jnp.bfloat16)
    conv_two = causal_conv(normed_two, kernel_two, bias_two, prev_one, prev_two)
    decoded = (frames.astype(jnp.float32) + conv_two.astype(jnp.float32)) * live_float
    return decoded.astype(jnp.bfloat16)
```

```python
import functools

import jax
import jax.numpy as jnp
from jax import lax
from jax.experimental import pallas as pl
from jax.experimental.pallas import tpu as pltpu
from jax.sharding import PartitionSpec as P

GROUPS = 32
EPS = 1e-05
LANES = 128
MESH = pl.DeviceIdType.MESH
F32 = jnp.float32
BF16 = jnp.bfloat16
HIGHEST = lax.Precision.HIGHEST


def silu(v):
    half = 0.5 * v
    return half + half * jnp.tanh(half)


def lane_roll(v, shift):
    shift = shift % LANES
    return v if shift == 0 else pltpu.roll(v, shift, v.ndim - 1)


def place_lanes(pieces, width):
    if len(pieces) == 1:
        return pieces[0]
    block = lax.broadcasted_iota(jnp.int32, pieces[0].shape, pieces[0].ndim - 1) // width
    out = pieces[-1]
    for i in range(len(pieces) - 2, -1, -1):
        out = jnp.where(block == i, pieces[i], out)
    return out


def block_kernel(
    sizes,
    frames_ref, counts_ref, k1_ref, k2_ref, g1_ref, o1_ref, b1_ref, g2_ref, o2_ref, b2_ref,
    out_ref,
    xraw, xn, k1v, k2v, pk, part, zsend, zrecv, csend, rret,
    local_sem, gs_sem, gr_sem, fs_sem, zs_sem, zr_sem, as_sem, ar_sem,
):
    G, S, F, H, W, C, wo, npad, pack, hp = sizes
    g = lax.axis_index("span")
    me = lax.axis_index("space")
    core = me % 2
    chip = me // 2
    chips = S // 2
    sib = chip * 2 + (1 - core)
    cols = C // LANES
    cpg = C // GROUPS

    def ident(dev):
        return (g, dev)

    for i, (src, dst) in enumerate(((k1_ref, k1v), (k2_ref, k2v))):
        pltpu.make_async_copy(src, dst.at[:, 0:3 * wo], local_sem.at[i]).start()
    own = pltpu.make_async_copy(frames_ref, xraw.at[me], local_sem.at[2])
    own.start()

    zrecv[...] = jnp.zeros_like(zrecv)

    barrier = pltpu.get_barrier_semaphore()
    for k in range(1, S):
        pl.semaphore_signal(barrier, inc=1, device_id=ident((me + k) % S), device_id_type=MESH)
    for hop in (-2, -1, 1, 2):
        @pl.when((g + hop >= 0) & (g + hop < G))
        def _():
            pl.semaphore_signal(barrier, inc=1, device_id=(g + hop, me), device_id_type=MESH)
    others = jnp.minimum(g, 2) + jnp.minimum(G - 1 - g, 2)
    pl.semaphore_wait(barrier, S - 1 + others)

    def gather_copy(stage, src, buf, slot, dev, sem_at):
        return pltpu.make_async_remote_copy(
            src_ref=src, dst_ref=buf.at[slot],
            send_sem=gs_sem.at[stage, sem_at], recv_sem=gr_sem.at[stage, slot],
            device_id=ident(dev), device_id_type=MESH,
        )

    def gather_start(stage, src, buf):
        copies = []
        for k in range(1, chips):
            q = (chip + k) % chips
            copies.append(gather_copy(stage, src, buf, me, q * 2 + core, k))
        copies.append(gather_copy(stage, src, buf, me, sib, 0))
        for c in copies:
            c.start()
        return copies

    def gather_finish(stage, buf, copies, visit):
        def await_slot(slot):
            gather_copy(stage, buf.at[slot], buf, slot, sib, 0).wait_recv()

        await_slot(sib)
        visit(sib)
        forwards = []
        for k in range(1, chips):
            slot = ((chip + k) % chips) * 2 + core
            await_slot(slot)
            c = pltpu.make_async_remote_copy(
                src_ref=buf.at[slot], dst_ref=buf.at[slot],
                send_sem=fs_sem.at[stage, k], recv_sem=gr_sem.at[stage, slot],
                device_id=ident(sib), device_id_type=MESH,
            )
            c.start()
            forwards.append(c)
            visit(slot)
        for k in range(1, chips):
            slot = ((chip + k) % chips) * 2 + (1 - core)
            await_slot(slot)
            visit(slot)
        for c in copies + forwards:
            c.wait_send()

    copies = gather_start(0, frames_ref, xraw)

    xn[:, 0] = jnp.zeros((F, W, C), BF16)
    xn[:, H + 1] = jnp.zeros((F, W, C), BF16)
    if npad > 3 * wo:
        for dst in (k1v, k2v):
            dst[:, 3 * wo:npad] = jnp.zeros((9, npad - 3 * wo, C), BF16)

    count = counts_ref[g]
    own.wait()

    part[...] = jnp.zeros_like(part)

    def visit_row(slot):
        for f in range(F):
            v = xraw[slot, f].astype(F32).reshape(W // 8, 8, C)
            part[0, f] += jnp.sum(v, axis=0)
            part[1, f] += jnp.sum(v * v, axis=0)

    visit_row(me)
    gather_finish(0, xraw, copies, visit_row)

    members = float(H * W * cpg)
    row_id = lax.broadcasted_iota(jnp.int32, (LANES, LANES), 0)
    col_id = lax.broadcasted_iota(jnp.int32, (LANES, LANES), 1)

    def wide(ref):
        return jnp.concatenate([ref[j:j + 1, :] for j in range(cols)], axis=1)

    stats = jnp.concatenate(
        [jnp.sum(part[i, f], axis=0, keepdims=True) for i in range(2) for f in range(F)]
        + [jnp.zeros((8 - 2 * F, C), F32)], axis=0)
    tall = jnp.concatenate([stats[:, j * LANES:(j + 1) * LANES] for j in range(cols)], axis=0)
    same = (row_id // cpg == col_id // cpg).astype(F32)
    tall = jnp.dot(tall, same, precision=HIGHEST, preferred_element_type=F32)
    stats = jnp.concatenate([tall[j * 8:(j + 1) * 8] for j in range(cols)], axis=1) / members
    gain1 = wide(g1_ref)
    offset1 = wide(o1_ref)
    scales, shifts = [], []
    for f in range(F):
        average = stats[f:f + 1]
        spread = stats[F + f:F + f + 1] - average * average
        live = jnp.where(f < count, 1.0, 0.0)
        scale = lax.rsqrt(spread + EPS) * gain1
        scales.append(scale * live)
        shifts.append((offset1 - average * scale) * live)

    def norm_row(s, carry):
        for f in range(F):
            v = xraw[s, f].astype(F32)
            xn[f, 1 + s] = silu(v * scales[f] + shifts[f]).astype(BF16)
        return carry

    lax.fori_loop(0, S, norm_row, 0)

    tile = (me * wo) // LANES
    base = (me * wo) % LANES
    lane = lax.broadcasted_iota(jnp.int32, (1, LANES), 1)

    def own_lanes(ref):
        v = ref[pl.ds(tile, 1), :]
        v = jnp.where((lane >= base) & (lane < base + wo), v, 0.0)
        out = v
        for i in range(1, pack):
            out = out + lane_roll(v, i * wo)
        return out

    HW = H * W
    xpos = lax.broadcasted_iota(jnp.int32, (HW, LANES), 0) % W

    def packed(total):
        moved = []
        for j in range(3):
            at = (j * wo) // LANES * LANES
            t = total[:, at:at + LANES]
            if j == 0:
                t = jnp.where(xpos == 0, 0.0, pltpu.roll(t, 1, 0))
            elif j == 2:
                t = jnp.where(xpos == W - 1, 0.0, pltpu.roll(t, HW - 1, 0))
            moved.append(t)
        rows = HW // pack
        chunks = []
        for c in range(pack):
            acc = None
            for j in range(3):
                t = lane_roll(moved[j][c * rows:(c + 1) * rows], (c - j) * wo)
                acc = t if acc is None else acc + t
            chunks.append(acc)
        return place_lanes(chunks, wo)

    def taps(kv, dt):
        acc = None
        for dy in range(3):
            x = xn[:, dy:dy + H].reshape(F * HW, C)
            t = lax.dot_general(x, kv[dt * 3 + dy], (((1,), (1,)), ((), ())),
                                preferred_element_type=F32)
            acc = t if acc is None else acc + t
        return [acc[f * HW:(f + 1) * HW] for f in range(F)]

    def z_copies(stage):
        near = pltpu.make_async_remote_copy(
            src_ref=zsend.at[stage], dst_ref=zrecv.at[stage, 0:2],
            send_sem=zs_sem.at[stage, 0], recv_sem=zr_sem.at[stage, 0],
            device_id=(g + 1, me), device_id_type=MESH)
        far = pltpu.make_async_remote_copy(
            src_ref=zsend.at[stage, 1], dst_ref=zrecv.at[stage, 2],
            send_sem=zs_sem.at[stage, 1], recv_sem=zr_sem.at[stage, 1],
            device_id=(g + 2, me), device_id_type=MESH)
        return near, far

    def conv(stage, kv, bias):
        t0 = taps(kv, 0)
        t1 = taps(kv, 1)
        last0, last1 = t0[0], t1[0]
        second = jnp.zeros_like(t0[0])
        for f in range(1, F):
            last0 = jnp.where(f < count, t0[f], last0)
            last1 = jnp.where(f < count, t1[f], last1)
            second = jnp.where(f < count, t0[f - 1], second)
        zsend[stage, 0] = packed(last1 + second)
        zsend[stage, 1] = packed(last0)
        near, far = z_copies(stage)

        @pl.when(g + 1 < G)
        def _():
            near.start()

        @pl.when(g + 2 < G)
        def _():
            far.start()

        t2 = taps(kv, 2)
        outs = []
        for f in range(F):
            total = t2[f]
            if f >= 1:
                total = total + t1[f - 1]
            if f >= 2:
                total = total + t0[f - 2]
            outs.append(packed(total) + bias)

        @pl.when(g >= 1)
        def _():
            near.wait_recv()

        @pl.when(g >= 2)
        def _():
            far.wait_recv()

        alone = counts_ref[jnp.maximum(g - 1, 0)] < 2
        outs[0] = outs[0] + zrecv[stage, 0] + jnp.where(alone, zrecv[stage, 2], 0.0)
        outs[1] = outs[1] + zrecv[stage, 1]

        @pl.when(g + 1 < G)
        def _():
            near.wait_send()

        @pl.when(g + 2 < G)
        def _():
            far.wait_send()

        return [o.astype(BF16) for o in outs]

    pltpu.make_async_copy(k1_ref, k1v.at[:, 0:3 * wo], local_sem.at[0]).wait()
    conv1 = conv(0, k1v, own_lanes(b1_ref))

    wide1 = [v.astype(F32) for v in conv1]
    stats = jnp.concatenate(
        [jnp.sum(v, axis=0, keepdims=True) for v in wide1]
        + [jnp.sum(v * v, axis=0, keepdims=True) for v in wide1]
        + [jnp.zeros((8 - 2 * F, LANES), F32)], axis=0)
    same = ((row_id % wo) // cpg == (col_id % wo) // cpg).astype(F32)
    stats = jnp.dot(stats, same, precision=HIGHEST, preferred_element_type=F32) / members
    gain2 = own_lanes(g2_ref)
    offset2 = own_lanes(o2_ref)
    for f in range(F):
        average = stats[f:f + 1]
        spread = stats[F + f:F + f + 1] - average * average
        live = jnp.where(f < count, 1.0, 0.0)
        scale = lax.rsqrt(spread + EPS) * gain2
        shift = offset2 - average * scale
        pk[me, f] = silu(wide1[f] * (scale * live) + shift * live).astype(BF16)

    copies = gather_start(1, pk.at[me], pk)
    gather_finish(1, pk, copies, lambda slot: None)

    for j in range(cols):
        for f in range(F):
            loaded = [pk[j * pack + i, f].astype(F32) for i in range(pack)]
            for c in range(pack):
                v = place_lanes([lane_roll(loaded[i], (i - c) * wo) for i in range(pack)], wo)
                xn[f, 1 + c * hp:1 + (c + 1) * hp, :, j * LANES:(j + 1) * LANES] = (
                    v.astype(BF16).reshape(hp, W, LANES))

    pltpu.make_async_copy(k2_ref, k2v.at[:, 0:3 * wo], local_sem.at[1]).wait()
    conv2 = conv(1, k2v, own_lanes(b2_ref))
    for f in range(F):
        csend[:, f] = conv2[f].reshape(hp, W, LANES)

    def row_copy(dev, slot, k):
        return pltpu.make_async_remote_copy(
            src_ref=csend.at[dev % hp], dst_ref=rret.at[slot],
            send_sem=as_sem.at[k], recv_sem=ar_sem.at[slot],
            device_id=ident(dev), device_id_type=MESH)

    sends = [row_copy((me + k) % S, me, k) for k in range(1, S)]
    for c in sends:
        c.start()
    rret[me] = csend[me % hp]
    for k in range(1, S):
        row_copy((me + k) % S, (me + k) % S, k).wait_recv()
    chunk = me // hp
    for j in range(cols):
        pieces = [
            pltpu.roll(rret[j * pack + i].astype(F32).reshape(F * W, LANES),
                       ((i - chunk + pack) % pack) * wo, 1)
            for i in range(pack)
        ]
        out_ref[:, :, j * LANES:(j + 1) * LANES] = (
            place_lanes(pieces, wo).astype(BF16).reshape(F, W, LANES))
    for c in sends:
        c.wait_send()


def per_device(G, S, frames, counts, gain_one, offset_one, kernel_one, bias_one,
               gain_two, offset_two, kernel_two, bias_two):
    F, rows, W, C = frames.shape
    wo = kernel_one.shape[3]
    H = rows * S
    pack = LANES // wo
    hp = H // pack
    npad = -(-3 * wo // LANES) * LANES
    sizes = (G, S, F, H, W, C, wo, npad, pack, hp)
    live = (jnp.arange(F) < lax.dynamic_index_in_dim(
        counts, lax.axis_index("span"), keepdims=False)).astype(F32)

    def vec(v):
        return v.reshape(C // LANES, LANES)

    vmem = pl.BlockSpec(memory_space=pltpu.VMEM)
    hbm = pl.BlockSpec(memory_space=pl.ANY)
    returned = pl.pallas_call(
        functools.partial(block_kernel, sizes),
        out_shape=jax.ShapeDtypeStruct((F, W, C), BF16),
        in_specs=[hbm, pl.BlockSpec(memory_space=pltpu.SMEM), hbm, hbm] + [vmem] * 6,
        out_specs=vmem,
        scratch_shapes=[
            pltpu.VMEM((S, F, W, C), BF16),
            pltpu.VMEM((F, H + 2, W, C), BF16),
            pltpu.VMEM((9, npad, C), BF16),
            pltpu.VMEM((9, npad, C), BF16),
            pltpu.VMEM((S, F, hp * W, LANES), BF16),
            pltpu.VMEM((2, F, 8, C), F32),
            pltpu.VMEM((2, 2, hp * W, LANES), F32),
            pltpu.VMEM((2, 3, hp * W, LANES), F32),
            pltpu.VMEM((hp, F, W, LANES), BF16),
            pltpu.VMEM((S, F, W, LANES), BF16),
            pltpu.SemaphoreType.DMA((3,)),
            pltpu.SemaphoreType.DMA((2, S // 2)),
            pltpu.SemaphoreType.DMA((2, S)),
            pltpu.SemaphoreType.DMA((2, S // 2)),
            pltpu.SemaphoreType.DMA((2, 2)),
            pltpu.SemaphoreType.DMA((2, 2)),
            pltpu.SemaphoreType.DMA((S,)),
            pltpu.SemaphoreType.DMA((S,)),
        ],
        compiler_params=pltpu.CompilerParams(
            collective_id=0, has_side_effects=True, vmem_limit_bytes=56 * 1024 * 1024),
    )(
        frames.reshape(F, W, C), counts,
        kernel_one.reshape(9, 3 * wo, C), kernel_two.reshape(9, 3 * wo, C),
        vec(gain_one), vec(offset_one), vec(bias_one),
        vec(gain_two), vec(offset_two), vec(bias_two),
    )
    decoded = (frames.astype(F32) + returned.reshape(frames.shape).astype(F32)) * (
        live[:, None, None, None])
    return decoded.astype(BF16)


def solution(mesh):
    body = functools.partial(per_device, mesh.shape["span"], mesh.shape["space"])
    return jax.shard_map(
        body,
        mesh=mesh,
        in_specs=(
            P("span", "space", None, None), P(), P(), P(),
            P(None, None, None, "space", None), P(), P(), P(),
            P(None, None, None, "space", None), P(),
        ),
        out_specs=P("span", "space", None, None),
        check_vma=False,
    )
```

```python
import functools

import jax
import jax.numpy as jnp
from jax import lax
from jax.experimental import pallas as pl
from jax.experimental.pallas import tpu as pltpu
from jax.sharding import PartitionSpec as P

GROUPS = 32
EPS = 1e-05
LANES = 128
MESH = pl.DeviceIdType.MESH
F32 = jnp.float32
BF16 = jnp.bfloat16
HIGHEST = lax.Precision.HIGHEST


def silu(v):
    half = 0.5 * v
    return half + half * jnp.tanh(half)


def lane_roll(v, shift):
    shift = shift % LANES
    return v if shift == 0 else pltpu.roll(v, shift, v.ndim - 1)


def place_lanes(pieces, width):
    if len(pieces) == 1:
        return pieces[0]
    block = lax.broadcasted_iota(jnp.int32, pieces[0].shape, pieces[0].ndim - 1) // width
    out = pieces[-1]
    for i in range(len(pieces) - 2, -1, -1):
        out = jnp.where(block == i, pieces[i], out)
    return out


def block_kernel(
    sizes,
    frames_ref, counts_ref, k1_ref, k2_ref, g1_ref, o1_ref, b1_ref, g2_ref, o2_ref, b2_ref,
    out_ref,
    xown, xraw, xn, k1v, k2v, pk, zsend, zrecv, csend, rret,
    local_sem, gs_sem, gr_sem, fs_sem, zs_sem, zr_sem, as_sem, ar_sem,
):
    G, S, F, H, W, C, wo, npad, pack, hp = sizes
    g = lax.axis_index("span")
    me = lax.axis_index("space")
    core = me % 2
    chip = me // 2
    chips = S // 2
    sib = chip * 2 + (1 - core)
    cols = C // LANES
    cpg = C // GROUPS
    HW = H * W
    wq = W // pack

    def ident(dev):
        return (g, dev)

    own = pltpu.make_async_copy(frames_ref, xown, local_sem.at[2])
    own.start()
    weights = [
        pltpu.make_async_copy(src, dst.at[:, 0:3 * wo], local_sem.at[i])
        for i, (src, dst) in enumerate(((k1_ref, k1v), (k2_ref, k2v)))
    ]
    for w in weights:
        w.start()

    barrier = pltpu.get_barrier_semaphore()
    zrecv[...] = jnp.zeros_like(zrecv)
    for k in range(1, S):
        pl.semaphore_signal(barrier, inc=1, device_id=ident((me + k) % S), device_id_type=MESH)
    for hop in (-2, -1, 1, 2):
        @pl.when((g + hop >= 0) & (g + hop < G))
        def _():
            pl.semaphore_signal(barrier, inc=1, device_id=(g + hop, me), device_id_type=MESH)

    count = counts_ref[g]
    own.wait()
    for p in range(F):
        xraw[p, me] = xown[jnp.maximum(count - 1 - p, 0)]

    xn[:, 0] = jnp.zeros((F, W, C), BF16)
    xn[:, H + 1] = jnp.zeros((F, W, C), BF16)
    if npad > 3 * wo:
        for dst in (k1v, k2v):
            dst[:, 3 * wo:npad] = jnp.zeros((9, npad - 3 * wo, C), BF16)

    others = jnp.minimum(g, 2) + jnp.minimum(G - 1 - g, 2)
    pl.semaphore_wait(barrier, S - 1 + others)

    def peer(k):
        if chips % 2:
            return (chip + k) % chips
        return ((chip // 2 + k // 2) % (chips // 2)) * 2 + (chip % 2 + k % 2) % 2

    order = list(range(chips - 1, 0, -1))

    def block_copy(stage, buf, p, slot, dev, send):
        return pltpu.make_async_remote_copy(
            src_ref=buf.at[p, slot], dst_ref=buf.at[p, slot],
            send_sem=send, recv_sem=gr_sem.at[stage, p, slot],
            device_id=ident(dev), device_id_type=MESH,
        )

    def piece_start(stage, buf, p):
        copies = [
            block_copy(stage, buf, p, me, peer(k) * 2 + core, gs_sem.at[stage, p, k])
            for k in order
        ] + [block_copy(stage, buf, p, me, sib, gs_sem.at[stage, p, 0])]
        for c in copies:
            c.start()
        return copies

    def piece_finish(stage, buf, p):
        def await_slot(slot):
            block_copy(stage, buf, p, slot, sib, gs_sem.at[stage, p, 0]).wait_recv()

        forwards = []
        for k in reversed(order):
            slot = peer(k) * 2 + core
            await_slot(slot)
            c = block_copy(stage, buf, p, slot, sib, fs_sem.at[stage, p, k])
            c.start()
            forwards.append(c)
        await_slot(sib)
        for k in reversed(order):
            await_slot(peer(k) * 2 + (1 - core))
        return forwards

    started = []
    for p in range(F):
        started += piece_start(0, xraw, p)

    members = float(H * W * cpg)
    row_id = lax.broadcasted_iota(jnp.int32, (LANES, LANES), 0)
    col_id = lax.broadcasted_iota(jnp.int32, (LANES, LANES), 1)
    same_one = (row_id // cpg == col_id // cpg).astype(F32)
    same_two = ((row_id % wo) // cpg == (col_id % wo) // cpg).astype(F32)

    def wide(ref):
        return jnp.concatenate([ref[j:j + 1, :] for j in range(cols)], axis=1)

    gain1 = wide(g1_ref)
    offset1 = wide(o1_ref)

    tile = (me * wo) // LANES
    base = (me * wo) % LANES
    lane = lax.broadcasted_iota(jnp.int32, (1, LANES), 1)

    def own_lanes(ref):
        v = ref[pl.ds(tile, 1), :]
        v = jnp.where((lane >= base) & (lane < base + wo), v, 0.0)
        out = v
        for i in range(1, pack):
            out = out + lane_roll(v, i * wo)
        return out

    bias1, bias2 = own_lanes(b1_ref), own_lanes(b2_ref)
    gain2, offset2 = own_lanes(g2_ref), own_lanes(o2_ref)

    xpos = lax.broadcasted_iota(jnp.int32, (HW, LANES), 0) % W

    def norm_terms(sums, squares, gain, offset, p):
        average = sums / members
        spread = squares / members - average * average
        live = jnp.where(p < count, 1.0, 0.0)
        scale = lax.rsqrt(spread + EPS) * gain
        return scale * live, (offset - average * scale) * live

    def norm_one(p):
        def add_row(s, carry):
            v = xraw[p, s].astype(F32).reshape(W // 8, 8, C)
            return carry[0] + jnp.sum(v, axis=0), carry[1] + jnp.sum(v * v, axis=0)

        zero = jnp.zeros((8, C), F32)
        sums, squares = lax.fori_loop(0, S, add_row, (zero, zero), unroll=True)
        tall = jnp.concatenate(
            [t[:, j * LANES:(j + 1) * LANES] for t in (sums, squares) for j in range(cols)], axis=0)
        tall = jnp.sum(tall.reshape(2 * cols, 8, LANES), axis=1)
        tall = jnp.dot(tall, same_one, precision=HIGHEST, preferred_element_type=F32)
        sums = jnp.concatenate([tall[j:j + 1] for j in range(cols)], axis=1)
        squares = jnp.concatenate([tall[cols + j:cols + j + 1] for j in range(cols)], axis=1)
        scale, shift = norm_terms(sums, squares, gain1, offset1, p)

        def norm_row(s, carry):
            v = xraw[p, s].astype(F32)
            xn[p, 1 + s] = silu(v * scale + shift).astype(BF16)
            return carry

        lax.fori_loop(0, S, norm_row, 0, unroll=True)

    def unpack(p):
        for j in range(cols):
            loaded = [pk[p, j * pack + i].astype(F32) for i in range(pack)]
            for c in range(pack):
                v = place_lanes([lane_roll(loaded[i], (i - c) * wo) for i in range(pack)], wo)
                xn[p, 1 + c * hp:1 + (c + 1) * hp, :, j * LANES:(j + 1) * LANES] = (
                    v.astype(BF16).reshape(hp, W, LANES))

    def packed(total):
        moved = []
        for j in range(3):
            at = (j * wo) // LANES * LANES
            t = total[:, at:at + LANES]
            if j == 0:
                t = jnp.where(xpos == 0, 0.0, pltpu.roll(t, 1, 0))
            elif j == 2:
                t = jnp.where(xpos == W - 1, 0.0, pltpu.roll(t, HW - 1, 0))
            moved.append(t)
        rows = HW // pack
        chunks = []
        for c in range(pack):
            acc = None
            for j in range(3):
                t = lane_roll(moved[j][c * rows:(c + 1) * rows], (c - j) * wo)
                acc = t if acc is None else acc + t
            chunks.append(acc)
        return place_lanes(chunks, wo)

    def taps(kv, dt, p):
        acc = None
        for dy in range(3):
            x = xn[p, dy:dy + H].reshape(HW, C)
            t = lax.dot_general(x, kv[dt * 3 + dy], (((1,), (1,)), ((), ())),
                                preferred_element_type=F32)
            acc = t if acc is None else acc + t
        return acc

    def z_copy(stage, which):
        src, hop = ((0, 1), (1, 1), (1, 2))[which]
        return pltpu.make_async_remote_copy(
            src_ref=zsend.at[stage, src], dst_ref=zrecv.at[stage, which],
            send_sem=zs_sem.at[stage, which], recv_sem=zr_sem.at[stage, which],
            device_id=(g + hop, me), device_id_type=MESH)

    def z_start(stage, which):
        hop = (1, 1, 2)[which]

        @pl.when(g + hop < G)
        def _():
            z_copy(stage, which).start()

    def conv(stage, buf, kv, bias, prepare, emit):
        started = []
        sums = [None] * F
        near = None
        for p in range(F):
            started += piece_finish(stage, buf, p)
            prepare(p)
            if p == 0:
                weights[stage].wait()
                zsend[stage, 1] = packed(taps(kv, 0, 0))
                z_start(stage, 2)
                z_start(stage, 1)
                near = taps(kv, 1, 0)
            elif p == 1:
                t = taps(kv, 0, 1)
                zsend[stage, 0] = packed(near + t)
                z_start(stage, 0)
            for at in range(max(p - 2, 0), p + 1):
                dt = 2 - (p - at)
                t = taps(kv, dt, p)
                sums[at] = t if sums[at] is None else sums[at] + t
                if p == F - 1:
                    if at == 0:
                        for which, hop in ((1, 1), (2, 2), (0, 1)):
                            @pl.when(g >= hop)
                            def _():
                                z_copy(stage, which).wait_recv()
                        alone = counts_ref[jnp.maximum(g - 1, 0)] < 2
                        first = zrecv[stage, 0] + jnp.where(alone, zrecv[stage, 2], 0.0)
                        later = zrecv[stage, 1]
                    frame = count - 1 - at
                    cross = jnp.where(frame == 0, first, jnp.where(frame == 1, later, 0.0))
                    emit(at, (packed(sums[at]) + cross + bias).astype(BF16))
        for which, hop in ((1, 1), (2, 2), (0, 1)):
            @pl.when(g + hop < G)
            def _():
                z_copy(stage, which).wait_send()
        return started

    def norm_two(p, v):
        v = v.astype(F32)
        stats = jnp.concatenate(
            [jnp.sum(v, axis=0, keepdims=True), jnp.sum(v * v, axis=0, keepdims=True),
             jnp.zeros((6, LANES), F32)], axis=0)
        stats = jnp.dot(stats, same_two, precision=HIGHEST, preferred_element_type=F32)
        scale, shift = norm_terms(stats[0:1], stats[1:2], gain2, offset2, p)
        pk[p, me] = silu(v * scale + shift).astype(BF16)
        started.extend(piece_start(1, pk, p))

    started += conv(0, xraw, k1v, bias1, norm_one, norm_two)

    narrow = wq % 16 == 0

    def row_out(p, v):
        if not narrow:
            csend[:, p] = v.reshape(hp, W, LANES)
            return
        v = v.astype(F32)
        for d in range(S):
            c, r = d // hp, d % hp
            parts = [
                lane_roll(v[r * W + h * wq:r * W + (h + 1) * wq], (h - c) * wo)
                for h in range(pack)
            ]
            csend[d, p] = place_lanes(parts, wo).astype(BF16)

    started += conv(1, pk, k2v, bias2, unpack, row_out)

    def row_copy(dev, slot, k):
        return pltpu.make_async_remote_copy(
            src_ref=csend.at[dev if narrow else dev % hp], dst_ref=rret.at[slot],
            send_sem=as_sem.at[k], recv_sem=ar_sem.at[slot],
            device_id=ident(dev), device_id_type=MESH)

    sends = [row_copy((me + k) % S, me, k) for k in range(1, S)]
    for c in sends:
        c.start()
    rret[me] = csend[me if narrow else me % hp]
    for c in started:
        c.wait_send()
    for k in range(1, S):
        row_copy((me + k) % S, (me + k) % S, k).wait_recv()
    chunk = me // hp
    for j in range(cols):
        if narrow:
            got = [rret[j * pack + i].astype(F32).reshape(F * wq, LANES) for i in range(pack)]
            tiles = [
                place_lanes([lane_roll(got[i], (i - h) * wo) for i in range(pack)], wo)
                .reshape(F, wq, LANES)
                for h in range(pack)
            ]
            moved = [jnp.concatenate([t[p] for t in tiles], axis=0) for p in range(F)]
        else:
            got = place_lanes([
                pltpu.roll(rret[j * pack + i].astype(F32).reshape(F * W, LANES),
                           ((i - chunk + pack) % pack) * wo, 1)
                for i in range(pack)
            ], wo).reshape(F, W, LANES)
            moved = [got[p] for p in range(F)]
        at = slice(j * LANES, (j + 1) * LANES)
        for f in range(F):
            v = moved[0]
            for p in range(1, F):
                v = jnp.where(count - 1 - f == p, moved[p], v)
            v = xown[f, :, at].astype(F32) + v
            out_ref[f, :, at] = jnp.where(f < count, v, 0.0).astype(BF16)
    for c in sends:
        c.wait_send()


def per_device(G, S, frames, counts, gain_one, offset_one, kernel_one, bias_one,
               gain_two, offset_two, kernel_two, bias_two):
    F, rows, W, C = frames.shape
    wo = kernel_one.shape[3]
    H = rows * S
    pack = LANES // wo
    hp = H // pack
    npad = -(-3 * wo // LANES) * LANES
    sizes = (G, S, F, H, W, C, wo, npad, pack, hp)
    if (W // pack) % 16 == 0:
        row_block = [(S, F, W // pack, LANES)] * 2
    else:
        row_block = [(hp, F, W, LANES), (S, F, W, LANES)]
    def vec(v):
        return v.reshape(C // LANES, LANES)

    vmem = pl.BlockSpec(memory_space=pltpu.VMEM)
    hbm = pl.BlockSpec(memory_space=pl.ANY)
    decoded = pl.pallas_call(
        functools.partial(block_kernel, sizes),
        out_shape=jax.ShapeDtypeStruct((F, W, C), BF16),
        in_specs=[hbm, pl.BlockSpec(memory_space=pltpu.SMEM), hbm, hbm] + [vmem] * 6,
        out_specs=vmem,
        scratch_shapes=[
            pltpu.VMEM((F, W, C), BF16),
            pltpu.VMEM((F, S, W, C), BF16),
            pltpu.VMEM((F, H + 2, W, C), BF16),
            pltpu.VMEM((9, npad, C), BF16),
            pltpu.VMEM((9, npad, C), BF16),
            pltpu.VMEM((F, S, hp * W, LANES), BF16),
            pltpu.VMEM((2, 2, hp * W, LANES), F32),
            pltpu.VMEM((2, 3, hp * W, LANES), F32),
            pltpu.VMEM(row_block[0], BF16),
            pltpu.VMEM(row_block[1], BF16),
            pltpu.SemaphoreType.DMA((3,)),
            pltpu.SemaphoreType.DMA((2, F, S // 2)),
            pltpu.SemaphoreType.DMA((2, F, S)),
            pltpu.SemaphoreType.DMA((2, F, S // 2)),
            pltpu.SemaphoreType.DMA((2, 3)),
            pltpu.SemaphoreType.DMA((2, 3)),
            pltpu.SemaphoreType.DMA((S,)),
            pltpu.SemaphoreType.DMA((S,)),
        ],
        compiler_params=pltpu.CompilerParams(
            collective_id=0, has_side_effects=True, vmem_limit_bytes=56 * 1024 * 1024),
    )(
        frames.reshape(F, W, C), counts,
        kernel_one.reshape(9, 3 * wo, C), kernel_two.reshape(9, 3 * wo, C),
        vec(gain_one), vec(offset_one), vec(bias_one),
        vec(gain_two), vec(offset_two), vec(bias_two),
    )
    return decoded.reshape(frames.shape)


def solution(mesh):
    body = functools.partial(per_device, mesh.shape["span"], mesh.shape["space"])
    return jax.shard_map(
        body,
        mesh=mesh,
        in_specs=(
            P("span", "space", None, None), P(), P(), P(),
            P(None, None, None, "space", None), P(), P(), P(),
            P(None, None, None, "space", None), P(),
        ),
        out_specs=P("span", "space", None, None),
        check_vma=False,
    )
```
